32 devices in a mesh: segment: 2 (over x), tensor: 16 (over z, y, core).
Axes of the slice: x: 2, y: 2, z: 4, core: 2. Of those that a mesh axis runs over, the one named last changes fastest.
Arguments:
- step_inputs: bfloat16 [3, 16, 8192], P(None, None, 'tensor'), may hold values from -6 to 6
- norm_gain: float32 [2, 8192], P('segment'), may hold values from 0.1 to 1.9
- query_weight: bfloat16 [2, 8192, 8192], P('segment', None, 'tensor'), may hold values from -0.0625 to 0.0625
- kv_weight: bfloat16 [2, 8192, 2, 1024], P('segment', None, None, 'tensor'), may hold values from -0.125 to 0.125
- out_weight: bfloat16 [2, 8192, 8192], P('segment', None, 'tensor'), may hold values from -0.125 to 0.125
- kv_cache: bfloat16 [2, 16, 3, 128, 256], P('segment', 'tensor'), as said below
- block_table: int32 [16, 2], replicated, may hold values from 0 to 2, as said below
- prefix_len: int32 [16], replicated, may hold values from 1 to 256, as said below
- parents: int32 [3, 16], replicated, may hold values from 0 to 15
Outputs:
- received: bfloat16 [2, 3, 16, 8192], P('segment', None, None, 'tensor')
The draws below stay inside these ranges and needn't reach their ends.
Inputs may be any that keep to these rules, and one draw needn't show every extreme that they name: `block_table`: every row of one source has the same first entry; its second entry is one of two blocks of that source, each of them used by some row; no block serves two sources. `prefix_len`: some row holds 256 tokens. `kv_cache`: copies c and c' are equal when c * 64 // (number of copies) // 8 equals the same for c'.
All inputs are finite; a program needn't handle non-finite values.
Results may differ from the reference program's by a relative error of at most 0.012.
The reference program's roundings to bfloat16 on the way count: a program that leaves them out, or rounds other values in their place, can miss the bound.
Values may be sent and summed in bfloat16 or wider, within the bound.
A program may use at most 64 MiB of HBM per device.

```python
import jax
import jax.numpy as jnp
from jax import lax

D = 8192
HEADS = 64
KV_HEADS = 8
HEAD_SIZE = 128
BEAMS = 16
BLOCK = 128
STEPS = 3
SOURCES = 1
GROUP = 8
ROWS = 16
BLOCKS = 3
N_SEGMENT = 2
N_TENSOR = 16


def draw_kv_cache(key, part):
    normal_key = jax.random.fold_in(key, 0)
    full_shape = (N_SEGMENT, KV_HEADS, BLOCKS, BLOCK, 2 * HEAD_SIZE)
    drawn = 2.0 * jax.random.normal(normal_key, full_shape, jnp.float32)
    kv_owner = jnp.arange(N_TENSOR) * (HEADS // N_TENSOR) // GROUP
    return jnp.take(drawn.astype(jnp.bfloat16), kv_owner, axis=1)


def draw_block_table(key, part):
    order_key, subtree_key = jax.random.split(key)
    pool_order = jax.random.permutation(order_key, BLOCKS).astype(jnp.int32).reshape(SOURCES, 3)
    subtree = jax.random.randint(subtree_key, (SOURCES, BEAMS), 0, 2)
    beam_index = jnp.arange(BEAMS)[None, :]
    subtree = jnp.where(beam_index == 0, 0, jnp.where(beam_index == 1, 1, subtree))
    first_slot = jnp.broadcast_to(pool_order[:, 0:1], (SOURCES, BEAMS))
    second = jnp.where(subtree == 0, pool_order[:, 1:2], pool_order[:, 2:3])
    return jnp.stack([first_slot, second], axis=-1).reshape(SOURCES * BEAMS, 2).astype(jnp.int32)


def draw_prefix_len(key, part):
    drawn = jax.random.randint(key, (SOURCES * BEAMS,), 1, 2 * BLOCK + 1)
    row_index = jnp.arange(SOURCES * BEAMS)
    return jnp.where(row_index == 0, 2 * BLOCK, drawn).astype(jnp.int32)


def set_ends(array, own_key, least, high):
    spot = [jax.random.randint(jax.random.fold_in(own_key, axis), (), 0, length) for axis, length in enumerate(array.shape)]
    longest = array.shape.index(max(array.shape))
    neighbour = spot[:longest] + [(spot[longest] + 1) % array.shape[longest]] + spot[longest + 1:]
    return array.at[tuple(spot)].set(least).at[tuple(neighbour)].set(high)


def block_scale(rng, shape, cuts, low, largest):
    loudness = 1.0
    for dim, parts in cuts:
        heights = jax.random.uniform(jax.random.fold_in(jax.random.fold_in(rng, 6), dim), (parts,), jnp.float32, low / len(cuts), largest / len(cuts))
        loudness = loudness * jnp.repeat(jnp.exp(heights), shape[dim] // parts).reshape((-1,) + (1,) * (len(shape) - 1 - dim))
    return loudness


def noise(rng, dims, spread, reach, cuts=(), held_as=jnp.bfloat16):
    level = block_scale(rng, dims, cuts, -0.22, 0.18) if cuts else 1.0
    values = jax.random.normal(rng, dims, jnp.float32) * spread * level
    return jnp.minimum(jnp.maximum(values, -reach), reach).astype(held_as)


def setup_inputs(seed: int = 0) -> dict:
    streams_of = jax.random.split(jax.random.key(seed), 10)
    return {
        "step_inputs": noise(streams_of[0], (STEPS, ROWS, D), 1.0, 6.0, ((2, 16),)),
        "norm_gain": jnp.clip(1.0 + 0.18 * jax.random.normal(streams_of[1], (N_SEGMENT, D), jnp.float32), 0.1, 1.9),
        "query_weight": noise(streams_of[2], (N_SEGMENT, D, HEADS * HEAD_SIZE), D ** -0.5, 0.0625, ((0, 2), (2, 16))),
        "kv_weight": noise(streams_of[3], (N_SEGMENT, D, 2, KV_HEADS * HEAD_SIZE), (D // 4) ** -0.5, 0.125, ((0, 2), (3, 16))),
        "out_weight": noise(streams_of[4], (N_SEGMENT, HEADS * HEAD_SIZE, D), (HEADS * HEAD_SIZE // 4) ** -0.5, 0.125, ((0, 2), (2, 16))),
        "kv_cache": draw_kv_cache(jax.random.fold_in(streams_of[9], 71), 0),
        "block_table": draw_block_table(jax.random.fold_in(streams_of[9], 71), 0),
        "prefix_len": draw_prefix_len(jax.random.fold_in(streams_of[9], 71), 0),
        "parents": set_ends(jax.random.randint(streams_of[8], (STEPS, ROWS), 0, BEAMS), jax.random.fold_in(streams_of[8], 1), 0, BEAMS - 1).astype(jnp.int32),
    }


ROPE_BASE = 1000000.0
NORM_EPS = 1e-06
MASK_FLOOR = -1e+30

def normalize(rows_in, gain):
    widened = rows_in.astype(jnp.float32)
    mean_square = lax.optimization_barrier(jnp.mean(widened * widened, axis=-1, keepdims=True))
    return (widened * lax.rsqrt(mean_square + NORM_EPS) * gain).astype(jnp.bfloat16)

def rotate(values, positions):
    half_size = values.shape[-1] // 2
    exponent = jnp.arange(half_size, dtype=jnp.float32) * (2.0 / values.shape[-1])
    frequency = jnp.power(jnp.float32(ROPE_BASE), -exponent)
    angles = positions.astype(jnp.float32)[:, None] * frequency[None, :]
    angles = jnp.concatenate([angles, angles], axis=-1)[:, None, :]
    front_part = values[..., :half_size]
    back_part = values[..., half_size:]
    turned = jnp.concatenate([-back_part, front_part], axis=-1)
    return values * jnp.cos(angles) + turned * jnp.sin(angles)

def ancestry(parents):
    rows_all = parents.shape[1]
    source_start = jnp.arange(rows_all, dtype=jnp.int32) // BEAMS * BEAMS
    lineage = []
    root_table = []
    for later_step in range(STEPS):
        current = jnp.arange(rows_all, dtype=jnp.int32)
        lineage_list = [current]
        for earlier in range(later_step, 0, -1):
            current = source_start + parents[earlier][current]
            lineage_list.append(current)
        lineage_list = lineage_list[::-1] + [current] * (STEPS - later_step - 1)
        lineage.append(jnp.stack(lineage_list))
        root_table.append(source_start + parents[0][current])
    return (jnp.stack(lineage), jnp.stack(root_table))

def reference(step_inputs, norm_gain, query_weight, kv_weight, out_weight, kv_cache, block_table, prefix_len, parents):
    lineage, root_table = ancestry(parents)
    rows_all = step_inputs.shape[1]
    head_dev = HEADS // N_TENSOR
    score_scale = HEAD_SIZE ** (-0.5)
    residual = step_inputs
    outputs = []
    for segment_index in range(N_SEGMENT):
        normed = normalize(residual.reshape(STEPS * rows_all, D), norm_gain[segment_index])
        queries = jnp.dot(normed, query_weight[segment_index], preferred_element_type=jnp.float32)
        queries = queries.reshape(STEPS, rows_all, HEADS, HEAD_SIZE)
        projected = jnp.dot(normed, kv_weight[segment_index].reshape(D, 2 * KV_HEADS * HEAD_SIZE), preferred_element_type=jnp.float32)
        projected = projected.astype(jnp.bfloat16).reshape(STEPS, rows_all, 2, HEAD_SIZE, KV_HEADS)
        projected = jnp.transpose(projected, (0, 1, 2, 4, 3))
        new_keys = []
        turned_queries = []
        for step_index in range(STEPS):
            positions = prefix_len[root_table[step_index]] + step_index
            new_keys.append(rotate(projected[step_index, :, 0].astype(jnp.float32), positions).astype(jnp.bfloat16))
            turned_queries.append(rotate(queries[step_index], positions).astype(jnp.bfloat16))
        new_keys = jnp.stack(new_keys)
        new_values = projected[:, :, 1]
        attended_steps = []
        for step_index in range(STEPS):
            root_rows = root_table[step_index]
            lengths = prefix_len[root_rows]
            prefix_mask = jnp.arange(2 * BLOCK, dtype=jnp.int32)[None, :] < lengths[:, None]
            history_mask = jnp.arange(STEPS, dtype=jnp.int32) <= step_index
            table_rows = block_table[root_rows]
            heads_out = []
            for kv_index in range(KV_HEADS):
                copy_index = kv_index * GROUP // head_dev
                blocks = kv_cache[segment_index, copy_index][table_rows]
                blocks = blocks.reshape(rows_all, 2 * BLOCK, 2 * HEAD_SIZE).astype(jnp.float32)
                history_keys = jnp.stack([new_keys[earlier, lineage[step_index, earlier], kv_index] for earlier in range(STEPS)], axis=1).astype(jnp.float32)
                history_values = jnp.stack([new_values[earlier, lineage[step_index, earlier], kv_index] for earlier in range(STEPS)], axis=1).astype(jnp.float32)
                group_queries = turned_queries[step_index][:, kv_index * GROUP:(kv_index + 1) * GROUP].astype(jnp.float32)
                prefix_scores = jnp.einsum('rhd,rkd->rhk', group_queries, blocks[:, :, :HEAD_SIZE]) * score_scale
                prefix_scores = jnp.where(prefix_mask[:, None, :], prefix_scores, MASK_FLOOR)
                history_scores = jnp.einsum('rhd,rtd->rht', group_queries, history_keys) * score_scale
                history_scores = jnp.where(history_mask[None, None, :], history_scores, MASK_FLOOR)
                highest = jnp.maximum(lax.optimization_barrier(jnp.max(prefix_scores, axis=-1)), lax.optimization_barrier(jnp.max(history_scores, axis=-1)))[..., None]
                prefix_exp = jnp.exp(prefix_scores - highest)
                history_exp = jnp.exp(history_scores - highest)
                denominator = lax.optimization_barrier(jnp.sum(prefix_exp, axis=-1, keepdims=True)) + lax.optimization_barrier(jnp.sum(history_exp, axis=-1, keepdims=True))
                prefix_probs = lax.optimization_barrier((prefix_exp / denominator).astype(jnp.bfloat16)).astype(jnp.float32)
                history_probs = lax.optimization_barrier((history_exp / denominator).astype(jnp.bfloat16)).astype(jnp.float32)
                mixture = jnp.einsum('rhk,rkd->rhd', prefix_probs, blocks[:, :, HEAD_SIZE:])
                mixture = mixture + jnp.einsum('rht,rtd->rhd', history_probs, history_values)
                heads_out.append(mixture)
            attended_steps.append(jnp.concatenate(heads_out, axis=1).reshape(rows_all, HEADS * HEAD_SIZE))
        attended = jnp.stack(attended_steps).astype(jnp.bfloat16).reshape(STEPS * rows_all, HEADS * HEAD_SIZE)
        update = jnp.dot(attended, out_weight[segment_index], preferred_element_type=jnp.float32).reshape(STEPS, rows_all, D)
        residual = (residual.astype(jnp.float32) + update).astype(jnp.bfloat16)
        outputs.append(residual)
    return jnp.stack([outputs[-1]] + outputs[:-1])
```

```python
import functools

import jax
import jax.numpy as jnp
from jax import lax
from jax.experimental import pallas as pl
from jax.experimental.pallas import tpu as pltpu
from jax.sharding import PartitionSpec as P

KV_HEADS = 8
HEAD_SIZE = 128
BEAMS = 16
BLOCK = 128
GROUP = 8
ROPE_BASE = 1000000.0
NORM_EPS = 1e-06
MASK_FLOOR = -1e30
MESH = pl.DeviceIdType.MESH
CORES = 2
COLUMNS = 2


def dot(a, b):
    return jnp.dot(a, b, preferred_element_type=jnp.float32)


def dot_nt(a, b):
    return lax.dot_general(a, b, (((1,), (1,)), ((), ())), preferred_element_type=jnp.float32)


class Gather:
    def __init__(self, buf, send, recv, me, lines):
        self.buf, self.send, self.recv, self.lines = buf, send, recv, lines
        self.me = me
        self.a = me // (COLUMNS * CORES)
        self.b = (me // CORES) % COLUMNS
        self.c = me % CORES
        self.started = []

    def slot(self, a, b, c):
        return (a * COLUMNS + b) * CORES + c

    def line(self, i):
        return lax.rem(self.a + i, self.lines)

    def peers(self):
        found = [self.slot(self.line(i), self.b, self.c) for i in range(1, self.lines)]
        return found + [self.across(), self.sibling()]

    def across(self):
        return self.slot(self.a, 1 - self.b, self.c)

    def sibling(self):
        return self.slot(self.a, self.b, 1 - self.c)

    def push(self, slot, target):
        copy = pltpu.make_async_remote_copy(
            src_ref=self.buf.at[slot],
            dst_ref=self.buf.at[slot],
            send_sem=self.send.at[len(self.started)],
            recv_sem=self.recv.at[slot],
            device_id={"tensor": target},
            device_id_type=MESH,
        )
        copy.start()
        self.started.append(copy)

    def arrived(self, slot):
        pltpu.make_async_remote_copy(
            src_ref=self.buf.at[slot],
            dst_ref=self.buf.at[slot],
            send_sem=self.send.at[0],
            recv_sem=self.recv.at[slot],
            device_id={"tensor": self.sibling()},
            device_id_type=MESH,
        ).wait_recv()

    def first(self, use):
        for peer in self.peers():
            self.push(self.me, peer)
        use(self.me)

    def second(self, use):
        for i in [1, self.lines - 1] + list(range(2, self.lines - 1)):
            slot = self.slot(self.line(i), self.b, self.c)
            self.arrived(slot)
            self.push(slot, self.across())
            self.push(slot, self.sibling())
            use(slot)

    def third(self, use):
        for i in [0, 1, self.lines - 1] + list(range(2, self.lines - 1)):
            slot = self.slot(self.line(i), 1 - self.b, self.c)
            self.arrived(slot)
            self.push(slot, self.sibling())
            use(slot)

    def fourth(self, use):
        for b in (self.b, 1 - self.b):
            for i in [0, 1, self.lines - 1] + list(range(2, self.lines - 1)):
                slot = self.slot(self.line(i), b, 1 - self.c)
                self.arrived(slot)
                use(slot)

    def finish(self):
        for copy in self.started:
            copy.wait_send()


def visible(meta, steps, rows, blocks):
    lane = lax.broadcasted_iota(jnp.int32, (rows, rows), 1)
    eye = (lane == lax.broadcasted_iota(jnp.int32, (rows, rows), 0)).astype(jnp.float32)
    picks = [(meta[:, t : t + 1] == lane.astype(jnp.float32)).astype(jnp.float32) for t in range(steps)]
    token = lax.broadcasted_iota(jnp.int32, (rows, blocks * BLOCK), 1)
    block = (token // BLOCK).astype(jnp.float32)
    offset = (token % BLOCK).astype(jnp.float32)
    place = lax.broadcasted_iota(jnp.int32, (rows, steps * rows), 1)
    own = lax.broadcasted_iota(jnp.int32, (rows, steps * rows), 0)
    cached, fresh, positions = [], [], []
    for step in range(steps):
        lineage = eye
        total = (place == own + step * rows).astype(jnp.float32)
        for earlier in range(step - 1, -1, -1):
            lineage = dot(lineage.astype(jnp.bfloat16), picks[earlier + 1].astype(jnp.bfloat16))
            spread = (place == own + earlier * rows).astype(jnp.bfloat16)
            total = total + dot(lineage.astype(jnp.bfloat16), spread)
        root = dot(lineage.astype(jnp.bfloat16), picks[0].astype(jnp.bfloat16))
        values = dot(root.astype(jnp.bfloat16), meta.astype(jnp.bfloat16))
        length = values[:, steps : steps + 1]
        count = jnp.zeros((rows, blocks * BLOCK), jnp.float32)
        for entry in range(2):
            named = values[:, steps + 1 + entry : steps + 2 + entry] == block
            inside = offset + float(entry * BLOCK) < length
            count = count + (named & inside).astype(jnp.float32)
        cached.append(count)
        fresh.append(total)
        positions.append(length + float(step))
    return jnp.concatenate(cached), jnp.concatenate(fresh), jnp.concatenate(positions)


def kernel(
    n, segments, steps,
    x_ref, gain_ref, meta_ref, freq_ref, wq_hbm, kv_hbm, wo_hbm, cache_hbm,
    out_ref,
    wq, kv, wo, cache, xbuf, nbuf, abuf, kvbuf, sel, inc, res,
    cached_ref, fresh_ref, cos_ref, sin_ref, total,
    load_sem, x_send, x_recv, k_send, k_recv, a_send, a_recv, hop_send, hop_recv,
):
    segment = lax.axis_index("segment")
    me = lax.axis_index("tensor")
    items, width = x_ref.shape
    rows = items // steps
    features = n * width
    blocks = cache.shape[0] // BLOCK
    lines = n // (COLUMNS * CORES)
    kv_columns = kv.shape[0] // 2
    channels = kv_columns // KV_HEADS
    heads = wq.shape[1] // HEAD_SIZE
    kv_head = me * heads // GROUP

    loads = [
        pltpu.make_async_copy(src, dst, load_sem.at[i])
        for i, (src, dst) in enumerate(((kv_hbm, kv), (wq_hbm, wq), (cache_hbm, cache), (wo_hbm, wo)))
    ]
    for load in loads:
        load.start()

    gx = Gather(xbuf, x_send, x_recv, me, lines)
    gk = Gather(kvbuf, k_send, k_recv, me, lines)
    ga = Gather(abuf, a_send, a_recv, me, lines)
    following = lax.rem(segment + 1, segments)
    before = lax.rem(segment + segments - 1, segments)

    barrier = pltpu.get_barrier_semaphore()
    peers = gx.peers()
    for peer in peers:
        pl.semaphore_signal(barrier, inc=1, device_id={"tensor": peer}, device_id_type=MESH)
    ends = [following] if segments == 2 else [following, before]
    for end in ends:
        pl.semaphore_signal(barrier, inc=1, device_id={"segment": end}, device_id_type=MESH)
    pl.semaphore_wait(barrier, len(peers) + len(ends))

    hop = pltpu.make_async_remote_copy(
        src_ref=res, dst_ref=inc, send_sem=hop_send, recv_sem=hop_recv,
        device_id={"segment": following}, device_id_type=MESH,
    )

    def prepare():
        cached, fresh, position = visible(meta_ref[...], steps, rows, blocks)
        cached_ref[...] = cached
        fresh_ref[...] = fresh
        angle = position * freq_ref[...]
        cos_ref[...] = jnp.cos(angle)
        half = lax.broadcasted_iota(jnp.int32, (items, HEAD_SIZE), 1) < HEAD_SIZE // 2
        sine = jnp.sin(angle)
        sin_ref[...] = jnp.where(half, -sine, sine)

        def fill(d, carry):
            line = lax.broadcasted_iota(jnp.int32, (2 * kv_columns, 2 * HEAD_SIZE), 0)
            column = lax.broadcasted_iota(jnp.int32, (2 * kv_columns, 2 * HEAD_SIZE), 1)
            inner = line % kv_columns
            goal = line // kv_columns * HEAD_SIZE + d * channels + inner // KV_HEADS
            hit = (inner % KV_HEADS == kv_head) & (column == goal)
            sel[d] = hit.astype(jnp.float32).astype(jnp.bfloat16)
            return carry

        lax.fori_loop(0, n, fill, 0)

    @pl.when(segment == 0)
    def _():
        xbuf[me] = x_ref[...]

    @pl.when(segment > 0)
    def _():
        prepare()
        hop.wait_recv()
        xbuf[me] = inc[...]

    def nothing(slot):
        pass

    total[...] = jnp.zeros_like(total)

    def squares(slot):
        chunk = xbuf[slot].astype(jnp.float32)
        total[...] += jnp.sum(chunk * chunk, axis=1, keepdims=True)

    gx.first(squares)

    @pl.when(segment == 0)
    def _():
        prepare()

    gx.second(squares)
    gx.third(squares)
    gx.fourth(squares)
    inverse = lax.rsqrt(total[...] * (1.0 / features) + NORM_EPS)

    loads[0].wait()

    def project_kv(s, acc):
        normed = (xbuf[s].astype(jnp.float32) * inverse * gain_ref[s]).astype(jnp.bfloat16)
        nbuf[s] = normed
        return acc + dot_nt(normed, kv[:, pl.ds(pl.multiple_of(s * width, width), width)])

    kv_own = lax.fori_loop(0, n, project_kv, jnp.zeros((items, 2 * kv_columns), jnp.float32))
    kvbuf[me] = kv_own.astype(jnp.bfloat16)
    gk.first(nothing)
    loads[1].wait()

    def project_q(s, acc):
        return acc + dot(nbuf[s], wq[pl.ds(pl.multiple_of(s * width, width), width), :])

    query = jnp.zeros((items, wq.shape[1]), jnp.float32)
    query = lax.fori_loop(0, n // 2, project_q, query)
    gk.second(nothing)
    query = lax.fori_loop(n // 2, n, project_q, query)
    gk.third(nothing)

    cos, sin = cos_ref[...], sin_ref[...]

    def rotated(values):
        return (values * cos + pltpu.roll(values, HEAD_SIZE // 2, 1) * sin).astype(jnp.bfloat16)

    turned = jnp.concatenate([rotated(query[:, h * HEAD_SIZE : (h + 1) * HEAD_SIZE]) for h in range(heads)])
    loads[2].wait()
    scale = HEAD_SIZE**-0.5
    keys = cache[:, :HEAD_SIZE]
    cached = jnp.concatenate([cached_ref[...]] * heads)
    fresh = jnp.concatenate([fresh_ref[...]] * heads)
    old_scores = jnp.where(cached > 0.0, dot_nt(turned, keys) * scale, MASK_FLOOR)
    gk.fourth(nothing)

    def collect(d, acc):
        return acc + dot(kvbuf[d], sel[d])

    entry = lax.fori_loop(0, n, collect, jnp.zeros((items, 2 * HEAD_SIZE), jnp.float32))
    new_key = rotated(entry[:, :HEAD_SIZE])
    new_value = entry[:, HEAD_SIZE:].astype(jnp.bfloat16)
    new_scores = jnp.where(fresh > 0.0, dot_nt(turned, new_key) * scale, MASK_FLOOR)
    highest = jnp.maximum(
        jnp.max(old_scores, axis=1, keepdims=True), jnp.max(new_scores, axis=1, keepdims=True)
    )
    old_exp = jnp.exp(old_scores - highest)
    new_exp = jnp.exp(new_scores - highest)
    denominator = jnp.sum(old_exp * cached, axis=1, keepdims=True) + jnp.sum(
        new_exp * fresh, axis=1, keepdims=True
    )
    old_probs = ((old_exp / denominator).astype(jnp.bfloat16).astype(jnp.float32) * cached).astype(jnp.bfloat16)
    new_probs = ((new_exp / denominator).astype(jnp.bfloat16).astype(jnp.float32) * fresh).astype(jnp.bfloat16)
    mixture = dot(old_probs, cache[:, HEAD_SIZE:]) + dot(new_probs, new_value)
    mixture = mixture.astype(jnp.bfloat16)
    for h in range(heads):
        abuf[me, :, h * HEAD_SIZE : (h + 1) * HEAD_SIZE] = mixture[h * items : (h + 1) * items]

    loads[3].wait()
    update = [xbuf[me].astype(jnp.float32), jnp.zeros((items, wo.shape[1]), jnp.float32)]

    def project_out(slot):
        update[1] = update[1] + dot(abuf[slot], wo[pl.ds(pl.multiple_of(slot * width, width), width), :])

    ga.first(project_out)
    ga.second(project_out)
    ga.third(project_out)
    ga.fourth(project_out)
    res[...] = (update[0] + update[1]).astype(jnp.bfloat16)
    hop.start()
    gx.finish()
    gk.finish()
    ga.finish()
    hop.wait_send()

    @pl.when(segment == 0)
    def _():
        hop.wait_recv()

    out_ref[...] = inc[...]


def per_device(
    n, segments, step_inputs, norm_gain, query_weight, kv_weight, out_weight, kv_cache, block_table, prefix_len, parents
):
    steps, rows, width = step_inputs.shape
    items = steps * rows
    kv_columns = kv_weight.shape[3]
    features = kv_weight.shape[1]
    blocks = kv_cache.shape[2]
    heads = query_weight.shape[2] // HEAD_SIZE
    start = jnp.arange(rows, dtype=jnp.int32)[:, None] // BEAMS * BEAMS
    meta = jnp.concatenate(
        [parents.T + start, prefix_len[:, None], block_table], axis=1
    ).astype(jnp.float32)
    exponent = jnp.arange(HEAD_SIZE // 2, dtype=jnp.float32) * (2.0 / HEAD_SIZE)
    frequency = jnp.power(jnp.float32(ROPE_BASE), -exponent)
    frequency = jnp.concatenate([frequency, frequency])[None, :]
    lines = n // (COLUMNS * CORES)
    sends = 4 * lines - 1
    bf16, f32 = jnp.bfloat16, jnp.float32
    vmem = pl.BlockSpec(memory_space=pltpu.VMEM)
    hbm = pl.BlockSpec(memory_space=pltpu.HBM)
    dma = pltpu.SemaphoreType.DMA
    received = pl.pallas_call(
        functools.partial(kernel, n, segments, steps),
        out_shape=jax.ShapeDtypeStruct((items, width), bf16),
        in_specs=[vmem] * 4 + [hbm] * 4,
        out_specs=vmem,
        scratch_shapes=[
            pltpu.VMEM((features, query_weight.shape[2]), bf16),
            pltpu.VMEM((2 * kv_columns, features), bf16),
            pltpu.VMEM((out_weight.shape[1], width), bf16),
            pltpu.VMEM((blocks * BLOCK, 2 * HEAD_SIZE), bf16),
            pltpu.VMEM((n, items, width), bf16),
            pltpu.VMEM((n, items, width), bf16),
            pltpu.VMEM((n, items, heads * HEAD_SIZE), bf16),
            pltpu.VMEM((n, items, 2 * kv_columns), bf16),
            pltpu.VMEM((n, 2 * kv_columns, 2 * HEAD_SIZE), bf16),
            pltpu.VMEM((items, width), bf16),
            pltpu.VMEM((items, width), bf16),
            pltpu.VMEM((items, blocks * BLOCK), f32),
            pltpu.VMEM((items, items), f32),
            pltpu.VMEM((items, HEAD_SIZE), f32),
            pltpu.VMEM((items, HEAD_SIZE), f32),
            pltpu.VMEM((items, 1), f32),
            dma((4,)),
            dma((sends,)), dma((n,)),
            dma((sends,)), dma((n,)),
            dma((sends,)), dma((n,)),
            dma, dma,
        ],
        compiler_params=pltpu.CompilerParams(
            collective_id=0, has_side_effects=True, vmem_limit_bytes=52 * 2**20
        ),
    )(
        step_inputs.reshape(items, width),
        norm_gain.reshape(n, 1, width),
        meta,
        frequency,
        query_weight[0],
        kv_weight[0].transpose(1, 2, 0).reshape(2 * kv_columns, features),
        out_weight[0],
        kv_cache.reshape(blocks * BLOCK, 2 * HEAD_SIZE),
    )
    return received.reshape(1, steps, rows, width)


def solution(mesh):
    return jax.shard_map(
        functools.partial(per_device, mesh.shape["tensor"], mesh.shape["segment"]),
        mesh=mesh,
        in_specs=(
            P(None, None, "tensor"),
            P("segment", None),
            P("segment", None, "tensor"),
            P("segment", None, None, "tensor"),
            P("segment", None, "tensor"),
            P("segment", "tensor", None, None, None),
            P(),
            P(),
            P(),
        ),
        out_specs=P("segment", None, None, "tensor"),
        check_vma=False,
    )
```

```python
import functools

import jax
import jax.numpy as jnp
from jax import lax
from jax.experimental import pallas as pl
from jax.experimental.pallas import tpu as pltpu
from jax.sharding import PartitionSpec as P

KV_HEADS = 8
HEAD_SIZE = 128
BEAMS = 16
BLOCK = 128
GROUP = 8
ROPE_BASE = 1000000.0
NORM_EPS = 1e-06
MASK_FLOOR = -1e30
MESH = pl.DeviceIdType.MESH
CORES = 2
COLUMNS = 2


def dot(a, b):
    return jnp.dot(a, b, preferred_element_type=jnp.float32)


def dot_nt(a, b):
    return lax.dot_general(a, b, (((1,), (1,)), ((), ())), preferred_element_type=jnp.float32)


class Gather:
    def __init__(self, buf, send, recv, me, lines):
        self.buf, self.send, self.recv, self.lines = buf, send, recv, lines
        self.me = me
        self.a = me // (COLUMNS * CORES)
        self.b = (me // CORES) % COLUMNS
        self.c = me % CORES
        self.started = []

    def slot(self, a, b, c):
        return (a * COLUMNS + b) * CORES + c

    def line(self, i):
        return lax.rem(self.a + i, self.lines)

    def peers(self):
        found = [self.slot(self.line(i), self.b, self.c) for i in range(1, self.lines)]
        return found + [self.across(), self.sibling()]

    def across(self):
        return self.slot(self.a, 1 - self.b, self.c)

    def sibling(self):
        return self.slot(self.a, self.b, 1 - self.c)

    def push(self, slot, target):
        copy = pltpu.make_async_remote_copy(
            src_ref=self.buf.at[slot],
            dst_ref=self.buf.at[slot],
            send_sem=self.send.at[len(self.started)],
            recv_sem=self.recv.at[slot],
            device_id={"tensor": target},
            device_id_type=MESH,
        )
        copy.start()
        self.started.append(copy)

    def arrived(self, slot):
        pltpu.make_async_remote_copy(
            src_ref=self.buf.at[slot],
            dst_ref=self.buf.at[slot],
            send_sem=self.send.at[0],
            recv_sem=self.recv.at[slot],
            device_id={"tensor": self.sibling()},
            device_id_type=MESH,
        ).wait_recv()

    def first(self, use):
        for peer in self.peers():
            self.push(self.me, peer)
        use(self.me)

    def second(self, use):
        for i in [1, self.lines - 1] + list(range(2, self.lines - 1)):
            slot = self.slot(self.line(i), self.b, self.c)
            self.arrived(slot)
            self.push(slot, self.across())
            self.push(slot, self.sibling())
            use(slot)

    def third(self, use):
        for i in [0, 1, self.lines - 1] + list(range(2, self.lines - 1)):
            slot = self.slot(self.line(i), 1 - self.b, self.c)
            self.arrived(slot)
            self.push(slot, self.sibling())
            use(slot)

    def fourth(self, use):
        for b in (self.b, 1 - self.b):
            for i in [0, 1, self.lines - 1] + list(range(2, self.lines - 1)):
                slot = self.slot(self.line(i), b, 1 - self.c)
                self.arrived(slot)
                use(slot)

    def finish(self):
        for copy in self.started:
            copy.wait_send()


def log2(size):
    return size.bit_length() - 1


def visible(listed, steps, rows, blocks):
    lane = lax.broadcasted_iota(jnp.int32, (rows, rows), 1)
    eye = (lane == lax.broadcasted_iota(jnp.int32, (rows, rows), 0)).astype(jnp.float32)
    meta = dot_nt(eye.astype(jnp.bfloat16), listed.astype(jnp.bfloat16))
    picks = [(meta[:, t : t + 1] == lane.astype(jnp.float32)).astype(jnp.float32) for t in range(steps)]
    token = lax.broadcasted_iota(jnp.int32, (rows, blocks * BLOCK), 1)
    block = (token >> log2(BLOCK)).astype(jnp.float32)
    offset = (token & (BLOCK - 1)).astype(jnp.float32)
    place = lax.broadcasted_iota(jnp.int32, (rows, steps * rows), 1)
    own = lax.broadcasted_iota(jnp.int32, (rows, steps * rows), 0)
    cached, fresh, positions = [], [], []
    for step in range(steps):
        lineage = eye
        total = (place == own + step * rows).astype(jnp.float32)
        for earlier in range(step - 1, -1, -1):
            lineage = dot(lineage.astype(jnp.bfloat16), picks[earlier + 1].astype(jnp.bfloat16))
            spread = (place == own + earlier * rows).astype(jnp.bfloat16)
            total = total + dot(lineage.astype(jnp.bfloat16), spread)
        root = dot(lineage.astype(jnp.bfloat16), picks[0].astype(jnp.bfloat16))
        values = dot(root.astype(jnp.bfloat16), meta.astype(jnp.bfloat16))
        length = values[:, steps : steps + 1]
        count = jnp.zeros((rows, blocks * BLOCK), jnp.float32)
        for entry in range(2):
            named = values[:, steps + 1 + entry : steps + 2 + entry] == block
            inside = offset + float(entry * BLOCK) < length
            count = count + (named & inside).astype(jnp.float32)
        cached.append(count)
        fresh.append(total)
        positions.append(length + float(step))
    return jnp.concatenate(cached), jnp.concatenate(fresh), jnp.concatenate(positions)


def kernel(
    n, segments, steps,
    meta_ref, freq_ref, x_hbm, gain_hbm, wq_hbm, kv_hbm, wo_hbm, cache_hbm,
    out_ref,
    gain_ref, wq, kv, wo, cache, xbuf, nbuf, abuf, kvbuf, sel, inc, res,
    cached_ref, fresh_ref, cos_ref, sin_ref, total,
    load_sem, x_send, x_recv, k_send, k_recv, a_send, a_recv, hop_send, hop_recv,
):
    segment = lax.axis_index("segment")
    me = lax.axis_index("tensor")
    items, width = x_hbm.shape
    rows = items // steps
    features = n * width
    blocks = cache.shape[0] // BLOCK
    lines = n // (COLUMNS * CORES)
    kv_columns = kv.shape[0] // 2
    channels = kv_columns // KV_HEADS
    heads = wq.shape[1] // HEAD_SIZE
    kv_head = me * heads // GROUP

    loads = [
        pltpu.make_async_copy(src, dst, load_sem.at[i])
        for i, (src, dst) in enumerate(
            (
                (x_hbm, xbuf.at[me]), (gain_hbm, gain_ref), (kv_hbm, kv),
                (wq_hbm, wq), (cache_hbm, cache), (wo_hbm, wo),
            )
        )
    ]
    for load in loads:
        load.start()

    gx = Gather(xbuf, x_send, x_recv, me, lines)
    gk = Gather(kvbuf, k_send, k_recv, me, lines)
    ga = Gather(abuf, a_send, a_recv, me, lines)
    following = lax.rem(segment + 1, segments)
    before = lax.rem(segment + segments - 1, segments)

    barrier = pltpu.get_barrier_semaphore()
    peers = gx.peers()
    for peer in peers:
        pl.semaphore_signal(barrier, inc=1, device_id={"tensor": peer}, device_id_type=MESH)
    ends = [following] if segments == 2 else [following, before]
    for end in ends:
        pl.semaphore_signal(barrier, inc=1, device_id={"segment": end}, device_id_type=MESH)
    pl.semaphore_wait(barrier, len(peers) + len(ends))

    hop = pltpu.make_async_remote_copy(
        src_ref=res, dst_ref=inc, send_sem=hop_send, recv_sem=hop_recv,
        device_id={"segment": following}, device_id_type=MESH,
    )

    def prepare_masks():
        cached, fresh, position = visible(meta_ref[...], steps, rows, blocks)
        cached_ref[...] = cached
        fresh_ref[...] = fresh
        cos_ref[...] = jnp.broadcast_to(position, cos_ref.shape)

    def prepare_turns():
        angle = cos_ref[...] * freq_ref[...]
        cos_ref[...] = jnp.cos(angle)
        half = lax.broadcasted_iota(jnp.int32, (items, HEAD_SIZE), 1) < HEAD_SIZE // 2
        sine = jnp.sin(angle)
        sin_ref[...] = jnp.where(half, -sine, sine)

    def prepare_picks():
        shape = (2 * kv_columns, 2 * HEAD_SIZE)
        line = lax.broadcasted_iota(jnp.int32, shape, 0)
        inner = line & (kv_columns - 1)
        goal = (line >> log2(kv_columns)) * HEAD_SIZE + (inner >> log2(KV_HEADS))
        goal = jnp.where((inner & (KV_HEADS - 1)) == kv_head, goal, -2 * HEAD_SIZE)
        ahead = lax.broadcasted_iota(jnp.int32, shape, 1) - goal

        def fill(d, carry):
            sel[d] = (ahead == d * channels).astype(jnp.float32).astype(jnp.bfloat16)
            return carry

        lax.fori_loop(0, n, fill, 0)

    def first_segment(part):
        @pl.when(segment == 0)
        def _():
            part()

    @pl.when(segment == 0)
    def _():
        loads[0].wait()

    @pl.when(segment > 0)
    def _():
        prepare_masks()
        prepare_turns()
        prepare_picks()
        with jax.named_scope("wait_hop"):
            loads[0].wait()
            hop.wait_recv()
            xbuf[me] = inc[...]

    def nothing(slot):
        pass

    total[...] = jnp.zeros_like(total)

    def squares(slot):
        chunk = xbuf[slot].astype(jnp.float32)
        total[...] += jnp.sum(chunk * chunk, axis=1, keepdims=True)

    with jax.named_scope("gather_rows"):
        gx.first(squares)
        first_segment(prepare_masks)
        gx.second(squares)
        first_segment(prepare_turns)
        gx.third(squares)
        first_segment(prepare_picks)
        gx.fourth(squares)
    inverse = lax.rsqrt(total[...] * (1.0 / features) + NORM_EPS)

    with jax.named_scope("normalize"):
        loads[1].wait()
        for s in range(n):
            normed = xbuf[s].astype(jnp.float32) * inverse * gain_ref[:, s * width : (s + 1) * width]
            nbuf[:, s * width : (s + 1) * width] = normed.astype(jnp.bfloat16)

    part = features // 4

    def project_q(i):
        return dot(nbuf[:, i * part : (i + 1) * part], wq[i * part : (i + 1) * part, :])

    with jax.named_scope("project_kv"):
        loads[2].wait()
        kv_own = dot_nt(nbuf[:, :part], kv[:, :part])
        for i in range(1, 4):
            kv_own = kv_own + dot_nt(nbuf[:, i * part : (i + 1) * part], kv[:, i * part : (i + 1) * part])
        kvbuf[me] = kv_own.astype(jnp.bfloat16)
        gk.first(nothing)
    with jax.named_scope("project_query"):
        loads[3].wait()
        query = project_q(0) + project_q(1)
        gk.second(nothing)
        query = query + project_q(2)
        gk.third(nothing)
        query = query + project_q(3)

    cos, sin = cos_ref[...], sin_ref[...]

    def rotated(values):
        return (values * cos + pltpu.roll(values, HEAD_SIZE // 2, 1) * sin).astype(jnp.bfloat16)

    turned = jnp.concatenate([rotated(query[:, h * HEAD_SIZE : (h + 1) * HEAD_SIZE]) for h in range(heads)])
    loads[4].wait()
    scale = HEAD_SIZE**-0.5
    keys = cache[:, :HEAD_SIZE]
    cached = jnp.concatenate([cached_ref[...]] * heads)
    fresh = jnp.concatenate([fresh_ref[...]] * heads)
    old_scores = jnp.where(cached > 0.0, dot_nt(turned, keys) * scale, MASK_FLOOR)
    with jax.named_scope("wait_kv"):
        gk.fourth(nothing)

    def collect(d, acc):
        return acc + dot(kvbuf[d], sel[d])

    entry = lax.fori_loop(0, n, collect, jnp.zeros((items, 2 * HEAD_SIZE), jnp.float32))
    new_key = rotated(entry[:, :HEAD_SIZE])
    new_value = entry[:, HEAD_SIZE:].astype(jnp.bfloat16)
    new_scores = jnp.where(fresh > 0.0, dot_nt(turned, new_key) * scale, MASK_FLOOR)
    highest = jnp.maximum(
        jnp.max(old_scores, axis=1, keepdims=True), jnp.max(new_scores, axis=1, keepdims=True)
    )
    old_exp = jnp.exp(old_scores - highest)
    new_exp = jnp.exp(new_scores - highest)
    denominator = jnp.sum(old_exp * cached, axis=1, keepdims=True) + jnp.sum(
        new_exp * fresh, axis=1, keepdims=True
    )
    old_probs = ((old_exp / denominator).astype(jnp.bfloat16).astype(jnp.float32) * cached).astype(jnp.bfloat16)
    new_probs = ((new_exp / denominator).astype(jnp.bfloat16).astype(jnp.float32) * fresh).astype(jnp.bfloat16)
    mixture = dot(old_probs, cache[:, HEAD_SIZE:]) + dot(new_probs, new_value)
    mixture = mixture.astype(jnp.bfloat16)
    for h in range(heads):
        abuf[me, :, h * HEAD_SIZE : (h + 1) * HEAD_SIZE] = mixture[h * items : (h + 1) * items]

    loads[5].wait()
    update = [xbuf[me].astype(jnp.float32), jnp.zeros((items, wo.shape[1]), jnp.float32)]

    def project_out(slot):
        update[1] = update[1] + dot(abuf[slot], wo[pl.ds(pl.multiple_of(slot * width, width), width), :])

    with jax.named_scope("gather_attended"):
        ga.first(project_out)
        ga.second(project_out)
        ga.third(project_out)
    with jax.named_scope("last_attended"):
        ga.fourth(project_out)
    res[...] = (update[0] + update[1]).astype(jnp.bfloat16)
    hop.start()
    gx.finish()
    gk.finish()
    ga.finish()
    hop.wait_send()

    @pl.when(segment == 0)
    def _():
        hop.wait_recv()

    out_ref[...] = inc[...]


def per_device(
    n, segments, step_inputs, norm_gain, query_weight, kv_weight, out_weight, kv_cache, block_table, prefix_len, parents
):
    steps, rows, width = step_inputs.shape
    items = steps * rows
    kv_columns = kv_weight.shape[3]
    features = kv_weight.shape[1]
    blocks = kv_cache.shape[2]
    heads = query_weight.shape[2] // HEAD_SIZE
    start = jnp.arange(rows, dtype=jnp.int32)[None, :] // BEAMS * BEAMS
    meta = jnp.concatenate(
        [parents + start, prefix_len[None, :], block_table.T], axis=0
    ).astype(jnp.float32)
    exponent = jnp.arange(HEAD_SIZE // 2, dtype=jnp.float32) * (2.0 / HEAD_SIZE)
    frequency = jnp.power(jnp.float32(ROPE_BASE), -exponent)
    frequency = jnp.concatenate([frequency, frequency])[None, :]
    lines = n // (COLUMNS * CORES)
    sends = 4 * lines - 1
    bf16, f32 = jnp.bfloat16, jnp.float32
    vmem = pl.BlockSpec(memory_space=pltpu.VMEM)
    hbm = pl.BlockSpec(memory_space=pltpu.HBM)
    dma = pltpu.SemaphoreType.DMA
    received = pl.pallas_call(
        functools.partial(kernel, n, segments, steps),
        out_shape=jax.ShapeDtypeStruct((items, width), bf16),
        in_specs=[vmem] * 2 + [hbm] * 6,
        out_specs=vmem,
        scratch_shapes=[
            pltpu.VMEM((1, features), f32),
            pltpu.VMEM((features, query_weight.shape[2]), bf16),
            pltpu.VMEM((2 * kv_columns, features), bf16),
            pltpu.VMEM((out_weight.shape[1], width), bf16),
            pltpu.VMEM((blocks * BLOCK, 2 * HEAD_SIZE), bf16),
            pltpu.VMEM((n, items, width), bf16),
            pltpu.VMEM((items, features), bf16),
            pltpu.VMEM((n, items, heads * HEAD_SIZE), bf16),
            pltpu.VMEM((n, items, 2 * kv_columns), bf16),
            pltpu.VMEM((n, 2 * kv_columns, 2 * HEAD_SIZE), bf16),
            pltpu.VMEM((items, width), bf16),
            pltpu.VMEM((items, width), bf16),
            pltpu.VMEM((items, blocks * BLOCK), f32),
            pltpu.VMEM((items, items), f32),
            pltpu.VMEM((items, HEAD_SIZE), f32),
            pltpu.VMEM((items, HEAD_SIZE), f32),
            pltpu.VMEM((items, 1), f32),
            dma((6,)),
            dma((sends,)), dma((n,)),
            dma((sends,)), dma((n,)),
            dma((sends,)), dma((n,)),
            dma, dma,
        ],
        compiler_params=pltpu.CompilerParams(
            collective_id=0, has_side_effects=True, vmem_limit_bytes=127 * 2**19
        ),
    )(
        meta,
        frequency,
        step_inputs.reshape(items, width),
        norm_gain,
        query_weight[0],
        kv_weight[0].transpose(1, 2, 0).reshape(2 * kv_columns, features),
        out_weight[0],
        kv_cache.reshape(blocks * BLOCK, 2 * HEAD_SIZE),
    )
    return received.reshape(1, steps, rows, width)


def solution(mesh):
    return jax.shard_map(
        functools.partial(per_device, mesh.shape["tensor"], mesh.shape["segment"]),
        mesh=mesh,
        in_specs=(
            P(None, None, "tensor"),
            P("segment", None),
            P("segment", None, "tensor"),
            P("segment", None, None, "tensor"),
            P("segment", None, "tensor"),
            P("segment", "tensor", None, None, None),
            P(),
            P(),
            P(),
        ),
        out_specs=P("segment", None, None, "tensor"),
        check_vma=False,
    )
```

```python
import functools
import math

import jax
import jax.numpy as jnp
from jax import lax
from jax.experimental import pallas as pl
from jax.experimental.pallas import tpu as pltpu
from jax.sharding import PartitionSpec as P

KV_HEADS = 8
HEAD_SIZE = 128
BEAMS = 16
BLOCK = 128
GROUP = 8
ROPE_BASE = 1000000.0
NORM_EPS = 1e-06
MASK_FLOOR = -1e30
MESH = pl.DeviceIdType.MESH
CORES = 2
COLUMNS = 2


def dot(a, b):
    return jnp.dot(a, b, preferred_element_type=jnp.float32)


def dot_nt(a, b):
    return lax.dot_general(a, b, (((1,), (1,)), ((), ())), preferred_element_type=jnp.float32)


class Gather:
    def __init__(self, buf, send, recv, me, lines):
        self.buf, self.send, self.recv, self.lines = buf, send, recv, lines
        self.me = me
        self.a = me // (COLUMNS * CORES)
        self.b = (me // CORES) % COLUMNS
        self.c = me % CORES
        self.started = []

    def slot(self, a, b, c):
        return (a * COLUMNS + b) * CORES + c

    def line(self, i):
        return lax.rem(self.a + i, self.lines)

    def peers(self):
        found = [self.slot(self.line(i), self.b, self.c) for i in range(1, self.lines)]
        return found + [self.across(), self.sibling()]

    def across(self):
        return self.slot(self.a, 1 - self.b, self.c)

    def sibling(self):
        return self.slot(self.a, self.b, 1 - self.c)

    def push(self, slot, target):
        copy = pltpu.make_async_remote_copy(
            src_ref=self.buf.at[slot],
            dst_ref=self.buf.at[slot],
            send_sem=self.send.at[len(self.started)],
            recv_sem=self.recv.at[slot],
            device_id={"tensor": target},
            device_id_type=MESH,
        )
        copy.start()
        self.started.append(copy)

    def arrived(self, slot):
        pltpu.make_async_remote_copy(
            src_ref=self.buf.at[slot],
            dst_ref=self.buf.at[slot],
            send_sem=self.send.at[0],
            recv_sem=self.recv.at[slot],
            device_id={"tensor": self.sibling()},
            device_id_type=MESH,
        ).wait_recv()

    def first(self, use):
        for peer in self.peers():
            self.push(self.me, peer)
        use(self.me)

    def second(self, use):
        for i in [1, self.lines - 1] + list(range(2, self.lines - 1)):
            slot = self.slot(self.line(i), self.b, self.c)
            self.arrived(slot)
            self.push(slot, self.across())
            self.push(slot, self.sibling())
            use(slot)

    def third(self, use):
        for i in [0, 1, self.lines - 1] + list(range(2, self.lines - 1)):
            slot = self.slot(self.line(i), 1 - self.b, self.c)
            self.arrived(slot)
            self.push(slot, self.sibling())
            use(slot)

    def fourth(self, use):
        for b in (self.b, 1 - self.b):
            for i in [0, 1, self.lines - 1] + list(range(2, self.lines - 1)):
                slot = self.slot(self.line(i), b, 1 - self.c)
                self.arrived(slot)
                use(slot)

    def finish(self):
        for copy in self.started:
            copy.wait_send()


def log2(size):
    return size.bit_length() - 1


def visible(listed, steps, rows, blocks):
    lane = lax.broadcasted_iota(jnp.int32, (rows, rows), 1)
    eye = (lane == lax.broadcasted_iota(jnp.int32, (rows, rows), 0)).astype(jnp.float32)
    meta = dot_nt(eye.astype(jnp.bfloat16), listed.astype(jnp.bfloat16))
    picks = [(meta[:, t : t + 1] == lane.astype(jnp.float32)).astype(jnp.float32) for t in range(steps)]
    token = lax.broadcasted_iota(jnp.int32, (rows, blocks * BLOCK), 1)
    block = (token >> log2(BLOCK)).astype(jnp.float32)
    offset = (token & (BLOCK - 1)).astype(jnp.float32)
    place = lax.broadcasted_iota(jnp.int32, (rows, steps * rows), 1)
    own = lax.broadcasted_iota(jnp.int32, (rows, steps * rows), 0)
    cached, fresh, positions = [], [], []
    for step in range(steps):
        lineage = eye
        total = (place == own + step * rows).astype(jnp.float32)
        for earlier in range(step - 1, -1, -1):
            lineage = dot(lineage.astype(jnp.bfloat16), picks[earlier + 1].astype(jnp.bfloat16))
            spread = (place == own + earlier * rows).astype(jnp.bfloat16)
            total = total + dot(lineage.astype(jnp.bfloat16), spread)
        root = dot(lineage.astype(jnp.bfloat16), picks[0].astype(jnp.bfloat16))
        values = dot(root.astype(jnp.bfloat16), meta.astype(jnp.bfloat16))
        length = values[:, steps : steps + 1]
        count = jnp.zeros((rows, blocks * BLOCK), jnp.float32)
        for entry in range(2):
            named = values[:, steps + 1 + entry : steps + 2 + entry] == block
            inside = offset + float(entry * BLOCK) < length
            count = count + (named & inside).astype(jnp.float32)
        cached.append(count)
        fresh.append(total)
        positions.append(length + float(step))
    return jnp.concatenate(cached), jnp.concatenate(fresh), jnp.concatenate(positions)


def kernel(
    n, segments, steps,
    x_hbm, gain_hbm, wq_hbm, kv_hbm, wo_hbm, cache_hbm, parents_hbm, length_hbm, table_hbm,
    out_ref,
    parents_ref, length_ref, table_ref, listed_ref, gain_ref, wq, kv, wo, cache, xbuf, nbuf, abuf, kvbuf, sel, inc, res,
    cached_ref, fresh_ref, cos_ref, sin_ref, total,
    load_sem, x_send, x_recv, k_send, k_recv, a_send, a_recv, hop_send, hop_recv,
):
    segment = lax.axis_index("segment")
    me = lax.axis_index("tensor")
    items, width = x_hbm.shape
    rows = items // steps
    features = n * width
    blocks = cache.shape[0] // BLOCK
    lines = n // (COLUMNS * CORES)
    kv_columns = kv.shape[0] // 2
    channels = kv_columns // KV_HEADS
    heads = wq.shape[1] // HEAD_SIZE
    kv_head = me * heads // GROUP

    loads = [
        pltpu.make_async_copy(src, dst, load_sem.at[i])
        for i, (src, dst) in enumerate(
            (
                (x_hbm, xbuf.at[me]), (gain_hbm, gain_ref), (kv_hbm, kv),
                (wq_hbm, wq), (cache_hbm, cache), (wo_hbm, wo),
                (parents_hbm, parents_ref), (length_hbm, length_ref), (table_hbm, table_ref),
            )
        )
    ]
    for load in loads:
        load.start()

    gx = Gather(xbuf, x_send, x_recv, me, lines)
    gk = Gather(kvbuf, k_send, k_recv, me, lines)
    ga = Gather(abuf, a_send, a_recv, me, lines)
    following = lax.rem(segment + 1, segments)
    before = lax.rem(segment + segments - 1, segments)

    barrier = pltpu.get_barrier_semaphore()
    peers = gx.peers()
    for peer in peers:
        pl.semaphore_signal(barrier, inc=1, device_id={"tensor": peer}, device_id_type=MESH)
    ends = [following] if segments == 2 else [following, before]
    for end in ends:
        pl.semaphore_signal(barrier, inc=1, device_id={"segment": end}, device_id_type=MESH)
    pl.semaphore_wait(barrier, len(peers) + len(ends))

    hop = pltpu.make_async_remote_copy(
        src_ref=res, dst_ref=inc, send_sem=hop_send, recv_sem=hop_recv,
        device_id={"segment": following}, device_id_type=MESH,
    )

    def prepare_masks():
        for load in loads[6:]:
            load.wait()
        base = (lax.broadcasted_iota(jnp.int32, (steps, rows), 1) >> log2(BEAMS)) << log2(BEAMS)
        listed_ref[0:steps] = (parents_ref[...] + base).astype(jnp.float32)
        listed_ref[steps : steps + 1] = length_ref[...].astype(jnp.float32)
        listed_ref[steps + 1 : steps + 3] = table_ref[...].astype(jnp.float32)
        cached, fresh, position = visible(listed_ref[...], steps, rows, blocks)
        cached_ref[...] = cached
        fresh_ref[...] = fresh
        cos_ref[...] = jnp.broadcast_to(position, cos_ref.shape)

    def prepare_turns():
        index = lax.broadcasted_iota(jnp.int32, (items, HEAD_SIZE), 1) & (HEAD_SIZE // 2 - 1)
        frequency = jnp.exp(index.astype(jnp.float32) * (-2.0 / HEAD_SIZE * math.log(ROPE_BASE)))
        angle = cos_ref[...] * frequency
        cos_ref[...] = jnp.cos(angle)
        half = lax.broadcasted_iota(jnp.int32, (items, HEAD_SIZE), 1) < HEAD_SIZE // 2
        sine = jnp.sin(angle)
        sin_ref[...] = jnp.where(half, -sine, sine)

    def prepare_picks():
        shape = (2 * kv_columns, 2 * HEAD_SIZE)
        line = lax.broadcasted_iota(jnp.int32, shape, 0)
        inner = line & (kv_columns - 1)
        goal = (line >> log2(kv_columns)) * HEAD_SIZE + (inner >> log2(KV_HEADS))
        goal = jnp.where((inner & (KV_HEADS - 1)) == kv_head, goal, -2 * HEAD_SIZE)
        ahead = lax.broadcasted_iota(jnp.int32, shape, 1) - goal

        def fill(d, carry):
            sel[d] = (ahead == d * channels).astype(jnp.float32).astype(jnp.bfloat16)
            return carry

        lax.fori_loop(0, n, fill, 0)

    def first_segment(part):
        @pl.when(segment == 0)
        def _():
            part()

    @pl.when(segment == 0)
    def _():
        loads[0].wait()

    @pl.when(segment > 0)
    def _():
        prepare_masks()
        prepare_turns()
        prepare_picks()
        with jax.named_scope("wait_hop"):
            loads[0].wait()
            hop.wait_recv()
            xbuf[me] = inc[...]

    def nothing(slot):
        pass

    total[...] = jnp.zeros_like(total)

    def squares(slot):
        chunk = xbuf[slot].astype(jnp.float32)
        total[...] += jnp.sum(chunk * chunk, axis=1, keepdims=True)

    with jax.named_scope("gather_rows"):
        gx.first(squares)
        first_segment(prepare_masks)
        gx.second(squares)
        first_segment(prepare_turns)
        gx.third(squares)
        first_segment(prepare_picks)
        gx.fourth(squares)
    inverse = lax.rsqrt(total[...] * (1.0 / features) + NORM_EPS)

    with jax.named_scope("normalize"):
        loads[1].wait()
        for s in range(n):
            normed = xbuf[s].astype(jnp.float32) * inverse * gain_ref[:, s * width : (s + 1) * width]
            nbuf[:, s * width : (s + 1) * width] = normed.astype(jnp.bfloat16)

    part = features // 4

    def project_q(i):
        return dot(nbuf[:, i * part : (i + 1) * part], wq[i * part : (i + 1) * part, :])

    with jax.named_scope("project_kv"):
        loads[2].wait()
        kv_own = dot_nt(nbuf[:, :part], kv[:, :part])
        for i in range(1, 4):
            kv_own = kv_own + dot_nt(nbuf[:, i * part : (i + 1) * part], kv[:, i * part : (i + 1) * part])
        kvbuf[me] = kv_own.astype(jnp.bfloat16)
        gk.first(nothing)
    with jax.named_scope("project_query"):
        loads[3].wait()
        query = project_q(0) + project_q(1)
        gk.second(nothing)
        query = query + project_q(2)
        gk.third(nothing)
        query = query + project_q(3)

    cos, sin = cos_ref[...], sin_ref[...]

    def rotated(values):
        return (values * cos + pltpu.roll(values, HEAD_SIZE // 2, 1) * sin).astype(jnp.bfloat16)

    turned = jnp.concatenate([rotated(query[:, h * HEAD_SIZE : (h + 1) * HEAD_SIZE]) for h in range(heads)])
    loads[4].wait()
    scale = HEAD_SIZE**-0.5
    keys = cache[:, :HEAD_SIZE]
    cached = jnp.concatenate([cached_ref[...]] * heads)
    fresh = jnp.concatenate([fresh_ref[...]] * heads)
    old_scores = jnp.where(cached > 0.0, dot_nt(turned, keys) * scale, MASK_FLOOR)
    with jax.named_scope("wait_kv"):
        gk.fourth(nothing)

    def collect(d, acc):
        return acc + dot(kvbuf[d], sel[d])

    entry = lax.fori_loop(0, n, collect, jnp.zeros((items, 2 * HEAD_SIZE), jnp.float32))
    new_key = rotated(entry[:, :HEAD_SIZE])
    new_value = entry[:, HEAD_SIZE:].astype(jnp.bfloat16)
    new_scores = jnp.where(fresh > 0.0, dot_nt(turned, new_key) * scale, MASK_FLOOR)
    highest = jnp.maximum(
        jnp.max(old_scores, axis=1, keepdims=True), jnp.max(new_scores, axis=1, keepdims=True)
    )
    old_exp = jnp.exp(old_scores - highest)
    new_exp = jnp.exp(new_scores - highest)
    denominator = jnp.sum(old_exp * cached, axis=1, keepdims=True) + jnp.sum(
        new_exp * fresh, axis=1, keepdims=True
    )
    old_probs = ((old_exp / denominator).astype(jnp.bfloat16).astype(jnp.float32) * cached).astype(jnp.bfloat16)
    new_probs = ((new_exp / denominator).astype(jnp.bfloat16).astype(jnp.float32) * fresh).astype(jnp.bfloat16)
    mixture = dot(old_probs, cache[:, HEAD_SIZE:]) + dot(new_probs, new_value)
    mixture = mixture.astype(jnp.bfloat16)
    for h in range(heads):
        abuf[me, :, h * HEAD_SIZE : (h + 1) * HEAD_SIZE] = mixture[h * items : (h + 1) * items]

    loads[5].wait()
    update = [xbuf[me].astype(jnp.float32), jnp.zeros((items, wo.shape[1]), jnp.float32)]

    def project_out(slot):
        update[1] = update[1] + dot(abuf[slot], wo[pl.ds(pl.multiple_of(slot * width, width), width), :])

    with jax.named_scope("gather_attended"):
        ga.first(project_out)
        waiting = []
        ga.second(waiting.append)
        ga.third(waiting.append)
        for slot in waiting:
            project_out(slot)
    with jax.named_scope("last_attended"):
        ga.fourth(project_out)
    res[...] = (update[0] + update[1]).astype(jnp.bfloat16)
    hop.start()
    gx.finish()
    gk.finish()
    ga.finish()
    hop.wait_send()

    @pl.when(segment == 0)
    def _():
        hop.wait_recv()

    out_ref[...] = inc[...]


def per_device(
    n, segments, step_inputs, norm_gain, query_weight, kv_weight, out_weight, kv_cache, block_table, prefix_len, parents
):
    steps, rows, width = step_inputs.shape
    items = steps * rows
    kv_columns = kv_weight.shape[3]
    features = kv_weight.shape[1]
    blocks = kv_cache.shape[2]
    heads = query_weight.shape[2] // HEAD_SIZE
    lines = n // (COLUMNS * CORES)
    sends = 4 * lines - 1
    bf16, f32 = jnp.bfloat16, jnp.float32
    vmem = pl.BlockSpec(memory_space=pltpu.VMEM)
    hbm = pl.BlockSpec(memory_space=pltpu.HBM)
    dma = pltpu.SemaphoreType.DMA
    received = pl.pallas_call(
        functools.partial(kernel, n, segments, steps),
        out_shape=jax.ShapeDtypeStruct((items, width), bf16),
        in_specs=[hbm] * 9,
        out_specs=vmem,
        scratch_shapes=[
            pltpu.VMEM((steps, rows), jnp.int32),
            pltpu.VMEM((1, rows), jnp.int32),
            pltpu.VMEM((2, rows), jnp.int32),
            pltpu.VMEM((steps + 3, rows), f32),
            pltpu.VMEM((1, features), f32),
            pltpu.VMEM((features, query_weight.shape[2]), bf16),
            pltpu.VMEM((2 * kv_columns, features), bf16),
            pltpu.VMEM((out_weight.shape[1], width), bf16),
            pltpu.VMEM((blocks * BLOCK, 2 * HEAD_SIZE), bf16),
            pltpu.VMEM((n, items, width), bf16),
            pltpu.VMEM((items, features), bf16),
            pltpu.VMEM((n, items, heads * HEAD_SIZE), bf16),
            pltpu.VMEM((n, items, 2 * kv_columns), bf16),
            pltpu.VMEM((n, 2 * kv_columns, 2 * HEAD_SIZE), bf16),
            pltpu.VMEM((items, width), bf16),
            pltpu.VMEM((items, width), bf16),
            pltpu.VMEM((items, blocks * BLOCK), f32),
            pltpu.VMEM((items, items), f32),
            pltpu.VMEM((items, HEAD_SIZE), f32),
            pltpu.VMEM((items, HEAD_SIZE), f32),
            pltpu.VMEM((items, 1), f32),
            dma((9,)),
            dma((sends,)), dma((n,)),
            dma((sends,)), dma((n,)),
            dma((sends,)), dma((n,)),
            dma, dma,
        ],
        compiler_params=pltpu.CompilerParams(
            collective_id=0, has_side_effects=True, vmem_limit_bytes=127 * 2**19
        ),
    )(
        step_inputs.reshape(items, width),
        norm_gain,
        query_weight[0],
        kv_weight[0].transpose(1, 2, 0).reshape(2 * kv_columns, features),
        out_weight[0],
        kv_cache.reshape(blocks * BLOCK, 2 * HEAD_SIZE),
        parents,
        prefix_len[None, :],
        block_table.T,
    )
    return received.reshape(1, steps, rows, width)


def solution(mesh):
    return jax.shard_map(
        functools.partial(per_device, mesh.shape["tensor"], mesh.shape["segment"]),
        mesh=mesh,
        in_specs=(
            P(None, None, "tensor"),
            P("segment", None),
            P("segment", None, "tensor"),
            P("segment", None, None, "tensor"),
            P("segment", None, "tensor"),
            P("segment", "tensor", None, None, None),
            P(),
            P(),
            P(),
        ),
        out_specs=P("segment", None, None, "tensor"),
        check_vma=False,
    )
```

```python
import functools
import math

import jax
import jax.numpy as jnp
from jax import lax
from jax.experimental import pallas as pl
from jax.experimental.pallas import tpu as pltpu
from jax.sharding import PartitionSpec as P

KV_HEADS = 8
HEAD_SIZE = 128
BEAMS = 16
BLOCK = 128
GROUP = 8
ROPE_BASE = 1000000.0
NORM_EPS = 1e-06
MASK_FLOOR = -1e30
MESH = pl.DeviceIdType.MESH
CORES = 2
COLUMNS = 2


def dot(a, b):
    return jnp.dot(a, b, preferred_element_type=jnp.float32)


def dot_nt(a, b):
    return lax.dot_general(a, b, (((1,), (1,)), ((), ())), preferred_element_type=jnp.float32)


class Gather:
    def __init__(self, buf, send, recv, me, lines):
        self.buf, self.send, self.recv, self.lines = buf, send, recv, lines
        self.me = me
        self.a = me // (COLUMNS * CORES)
        self.b = (me // CORES) % COLUMNS
        self.c = me % CORES
        self.started = []

    def slot(self, a, b, c):
        return (a * COLUMNS + b) * CORES + c

    def line(self, i):
        return lax.rem(self.a + i, self.lines)

    def peers(self):
        found = [self.slot(self.line(i), self.b, self.c) for i in range(1, self.lines)]
        return found + [self.across(), self.sibling()]

    def across(self):
        return self.slot(self.a, 1 - self.b, self.c)

    def sibling(self):
        return self.slot(self.a, self.b, 1 - self.c)

    def push(self, slot, target):
        copy = pltpu.make_async_remote_copy(
            src_ref=self.buf.at[slot],
            dst_ref=self.buf.at[slot],
            send_sem=self.send.at[len(self.started)],
            recv_sem=self.recv.at[slot],
            device_id={"tensor": target},
            device_id_type=MESH,
        )
        copy.start()
        self.started.append(copy)

    def arrived(self, slot):
        pltpu.make_async_remote_copy(
            src_ref=self.buf.at[slot],
            dst_ref=self.buf.at[slot],
            send_sem=self.send.at[0],
            recv_sem=self.recv.at[slot],
            device_id={"tensor": self.sibling()},
            device_id_type=MESH,
        ).wait_recv()

    def first(self, use):
        for peer in self.peers():
            self.push(self.me, peer)
        use(self.me)

    def second(self, use):
        for i in [1, self.lines - 1] + list(range(2, self.lines - 1)):
            slot = self.slot(self.line(i), self.b, self.c)
            self.arrived(slot)
            self.push(slot, self.across())
            self.push(slot, self.sibling())
            use(slot)

    def third(self, use):
        for i in [0, 1, self.lines - 1] + list(range(2, self.lines - 1)):
            slot = self.slot(self.line(i), 1 - self.b, self.c)
            self.arrived(slot)
            self.push(slot, self.sibling())
            use(slot)

    def fourth(self, use):
        for b in (self.b, 1 - self.b):
            for i in [0, 1, self.lines - 1] + list(range(2, self.lines - 1)):
                slot = self.slot(self.line(i), b, 1 - self.c)
                self.arrived(slot)
                use(slot)

    def finish(self):
        for copy in self.started:
            copy.wait_send()


def log2(size):
    return size.bit_length() - 1


def visible(listed, steps, rows, blocks):
    lane = lax.broadcasted_iota(jnp.int32, (rows, rows), 1)
    eye = (lane == lax.broadcasted_iota(jnp.int32, (rows, rows), 0)).astype(jnp.float32)
    meta = dot_nt(eye.astype(jnp.bfloat16), listed.astype(jnp.bfloat16))
    picks = [(meta[:, t : t + 1] == lane.astype(jnp.float32)).astype(jnp.float32) for t in range(steps)]
    token = lax.broadcasted_iota(jnp.int32, (rows, blocks * BLOCK), 1)
    block = (token >> log2(BLOCK)).astype(jnp.float32)
    offset = (token & (BLOCK - 1)).astype(jnp.float32)
    place = lax.broadcasted_iota(jnp.int32, (rows, steps * rows), 1)
    own = lax.broadcasted_iota(jnp.int32, (rows, steps * rows), 0)
    cached, fresh, positions = [], [], []
    for step in range(steps):
        lineage = eye
        total = (place == own + step * rows).astype(jnp.float32)
        for earlier in range(step - 1, -1, -1):
            lineage = dot(lineage.astype(jnp.bfloat16), picks[earlier + 1].astype(jnp.bfloat16))
            spread = (place == own + earlier * rows).astype(jnp.bfloat16)
            total = total + dot(lineage.astype(jnp.bfloat16), spread)
        root = dot(lineage.astype(jnp.bfloat16), picks[0].astype(jnp.bfloat16))
        values = dot(root.astype(jnp.bfloat16), meta.astype(jnp.bfloat16))
        length = values[:, steps : steps + 1]
        count = jnp.zeros((rows, blocks * BLOCK), jnp.float32)
        for entry in range(2):
            named = values[:, steps + 1 + entry : steps + 2 + entry] == block
            inside = offset + float(entry * BLOCK) < length
            count = count + (named & inside).astype(jnp.float32)
        cached.append(count)
        fresh.append(total)
        positions.append(length + float(step))
    return jnp.concatenate(cached), jnp.concatenate(fresh), jnp.concatenate(positions)


def kernel(
    n, segments, steps,
    x_hbm, gain_hbm, wq_hbm, kv_hbm, wo_hbm, cache_hbm, parents_hbm, length_hbm, table_hbm,
    out_ref,
    parents_ref, length_ref, table_ref, listed_ref, gain_ref, wq, kv, wo, cache, xbuf, nbuf, abuf, kvbuf, sel, inc, res,
    cached_ref, fresh_ref, cos_ref, sin_ref, total,
    load_sem, x_send, x_recv, k_send, k_recv, a_send, a_recv, hop_send, hop_recv,
):
    segment = lax.axis_index("segment")
    me = lax.axis_index("tensor")
    items, width = x_hbm.shape
    rows = items // steps
    features = n * width
    blocks = cache.shape[0] // BLOCK
    lines = n // (COLUMNS * CORES)
    kv_columns = kv.shape[0] // 2
    channels = kv_columns // KV_HEADS
    heads = wq.shape[1] // HEAD_SIZE
    kv_head = me * heads // GROUP

    loads = [
        pltpu.make_async_copy(src, dst, load_sem.at[i])
        for i, (src, dst) in enumerate(
            (
                (x_hbm, xbuf.at[me]), (gain_hbm, gain_ref), (kv_hbm, kv),
                (wq_hbm, wq), (cache_hbm, cache), (wo_hbm, wo),
                (parents_hbm, parents_ref), (length_hbm, length_ref), (table_hbm, table_ref),
            )
        )
    ]
    for load in loads:
        load.start()

    gx = Gather(xbuf, x_send, x_recv, me, lines)
    gk = Gather(kvbuf, k_send, k_recv, me, lines)
    ga = Gather(abuf, a_send, a_recv, me, lines)
    following = lax.rem(segment + 1, segments)
    before = lax.rem(segment + segments - 1, segments)

    barrier = pltpu.get_barrier_semaphore()
    peers = gx.peers()
    for peer in peers:
        pl.semaphore_signal(barrier, inc=1, device_id={"tensor": peer}, device_id_type=MESH)
    ends = [following] if segments == 2 else [following, before]
    for end in ends:
        pl.semaphore_signal(barrier, inc=1, device_id={"segment": end}, device_id_type=MESH)
    pl.semaphore_wait(barrier, len(peers) + len(ends))

    hop = pltpu.make_async_remote_copy(
        src_ref=res, dst_ref=inc, send_sem=hop_send, recv_sem=hop_recv,
        device_id={"segment": following}, device_id_type=MESH,
    )

    def prepare_masks():
        for load in loads[6:]:
            load.wait()
        base = (lax.broadcasted_iota(jnp.int32, (steps, rows), 1) >> log2(BEAMS)) << log2(BEAMS)
        listed_ref[0:steps] = (parents_ref[...] + base).astype(jnp.float32)
        listed_ref[steps : steps + 1] = length_ref[...].astype(jnp.float32)
        listed_ref[steps + 1 : steps + 3] = table_ref[...].astype(jnp.float32)
        cached, fresh, position = visible(listed_ref[...], steps, rows, blocks)
        cached_ref[...] = cached
        fresh_ref[...] = fresh
        cos_ref[...] = jnp.broadcast_to(position, cos_ref.shape)

    def prepare_turns():
        index = lax.broadcasted_iota(jnp.int32, (items, HEAD_SIZE), 1) & (HEAD_SIZE // 2 - 1)
        frequency = jnp.exp(index.astype(jnp.float32) * (-2.0 / HEAD_SIZE * math.log(ROPE_BASE)))
        angle = cos_ref[...] * frequency
        cos_ref[...] = jnp.cos(angle)
        half = lax.broadcasted_iota(jnp.int32, (items, HEAD_SIZE), 1) < HEAD_SIZE // 2
        sine = jnp.sin(angle)
        sin_ref[...] = jnp.where(half, -sine, sine)

    def prepare_picks():
        shape = (2 * kv_columns, 2 * HEAD_SIZE)
        line = lax.broadcasted_iota(jnp.int32, shape, 0)
        inner = line & (kv_columns - 1)
        goal = (line >> log2(kv_columns)) * HEAD_SIZE + (inner >> log2(KV_HEADS))
        goal = jnp.where((inner & (KV_HEADS - 1)) == kv_head, goal, -2 * HEAD_SIZE)
        ahead = lax.broadcasted_iota(jnp.int32, shape, 1) - goal

        def fill(d, carry):
            sel[d] = (ahead == d * channels).astype(jnp.float32).astype(jnp.bfloat16)
            return carry

        lax.fori_loop(0, n, fill, 0)

    def first_segment(part):
        @pl.when(segment == 0)
        def _():
            part()

    @pl.when(segment == 0)
    def _():
        loads[0].wait()

    @pl.when(segment > 0)
    def _():
        prepare_masks()
        prepare_turns()
        prepare_picks()
        with jax.named_scope("wait_hop"):
            loads[0].wait()
            hop.wait_recv()
            xbuf[me] = inc[...]

    def nothing(slot):
        pass

    total[...] = jnp.zeros_like(total)

    def squares(slot):
        chunk = xbuf[slot].astype(jnp.float32)
        total[...] += jnp.sum(chunk * chunk, axis=1, keepdims=True)

    with jax.named_scope("gather_rows"):
        gx.first(squares)
        early = []
        gx.second(early.append)
        gx.third(early.append)
        for slot in early:
            squares(slot)
        first_segment(prepare_masks)
        first_segment(prepare_turns)
        first_segment(prepare_picks)
        gx.fourth(squares)
    inverse = lax.rsqrt(total[...] * (1.0 / features) + NORM_EPS)

    with jax.named_scope("normalize"):
        loads[1].wait()
        for s in range(n):
            normed = xbuf[s].astype(jnp.float32) * inverse * gain_ref[:, s * width : (s + 1) * width]
            nbuf[:, s * width : (s + 1) * width] = normed.astype(jnp.bfloat16)

    part = features // 4

    def project_q(i):
        return dot(nbuf[:, i * part : (i + 1) * part], wq[i * part : (i + 1) * part, :])

    with jax.named_scope("project_kv"):
        loads[2].wait()
        kv_own = dot_nt(nbuf[:, :part], kv[:, :part])
        for i in range(1, 4):
            kv_own = kv_own + dot_nt(nbuf[:, i * part : (i + 1) * part], kv[:, i * part : (i + 1) * part])
        kvbuf[me] = kv_own.astype(jnp.bfloat16)
        gk.first(nothing)
    with jax.named_scope("project_query"):
        loads[3].wait()
        query = project_q(0) + project_q(1)
        gk.second(nothing)
        query = query + project_q(2)
        gk.third(nothing)
        query = query + project_q(3)

    cos, sin = cos_ref[...], sin_ref[...]

    def rotated(values):
        return (values * cos + pltpu.roll(values, HEAD_SIZE // 2, 1) * sin).astype(jnp.bfloat16)

    turned = jnp.concatenate([rotated(query[:, h * HEAD_SIZE : (h + 1) * HEAD_SIZE]) for h in range(heads)])
    loads[4].wait()
    scale = HEAD_SIZE**-0.5
    keys = cache[:, :HEAD_SIZE]
    cached = jnp.concatenate([cached_ref[...]] * heads)
    fresh = jnp.concatenate([fresh_ref[...]] * heads)
    old_scores = jnp.where(cached > 0.0, dot_nt(turned, keys) * scale, MASK_FLOOR)
    with jax.named_scope("wait_kv"):
        gk.fourth(nothing)

    def collect(d, acc):
        return acc + dot(kvbuf[d], sel[d])

    entry = lax.fori_loop(0, n, collect, jnp.zeros((items, 2 * HEAD_SIZE), jnp.float32))
    new_key = rotated(entry[:, :HEAD_SIZE])
    new_value = entry[:, HEAD_SIZE:].astype(jnp.bfloat16)
    new_scores = jnp.where(fresh > 0.0, dot_nt(turned, new_key) * scale, MASK_FLOOR)
    highest = jnp.maximum(
        jnp.max(old_scores, axis=1, keepdims=True), jnp.max(new_scores, axis=1, keepdims=True)
    )
    old_exp = jnp.exp(old_scores - highest)
    new_exp = jnp.exp(new_scores - highest)
    denominator = jnp.sum(old_exp * cached, axis=1, keepdims=True) + jnp.sum(
        new_exp * fresh, axis=1, keepdims=True
    )
    old_probs = ((old_exp / denominator).astype(jnp.bfloat16).astype(jnp.float32) * cached).astype(jnp.bfloat16)
    new_probs = ((new_exp / denominator).astype(jnp.bfloat16).astype(jnp.float32) * fresh).astype(jnp.bfloat16)
    mixture = dot(old_probs, cache[:, HEAD_SIZE:]) + dot(new_probs, new_value)
    mixture = mixture.astype(jnp.bfloat16)
    for h in range(heads):
        abuf[me, :, h * HEAD_SIZE : (h + 1) * HEAD_SIZE] = mixture[h * items : (h + 1) * items]

    loads[5].wait()
    update = [xbuf[me].astype(jnp.float32), jnp.zeros((items, wo.shape[1]), jnp.float32)]

    def project_out(slot):
        update[1] = update[1] + dot(abuf[slot], wo[pl.ds(pl.multiple_of(slot * width, width), width), :])

    with jax.named_scope("gather_attended"):
        ga.first(project_out)
        waiting = []
        ga.second(waiting.append)
        ga.third(waiting.append)
        for slot in waiting:
            project_out(slot)
    with jax.named_scope("last_attended"):
        ga.fourth(project_out)
    res[...] = (update[0] + update[1]).astype(jnp.bfloat16)
    hop.start()
    gx.finish()
    gk.finish()
    ga.finish()
    hop.wait_send()

    @pl.when(segment == 0)
    def _():
        hop.wait_recv()

    out_ref[...] = inc[...]


def per_device(
    n, segments, step_inputs, norm_gain, query_weight, kv_weight, out_weight, kv_cache, block_table, prefix_len, parents
):
    steps, rows, width = step_inputs.shape
    items = steps * rows
    kv_columns = kv_weight.shape[3]
    features = kv_weight.shape[1]
    blocks = kv_cache.shape[2]
    heads = query_weight.shape[2] // HEAD_SIZE
    lines = n // (COLUMNS * CORES)
    sends = 4 * lines - 1
    bf16, f32 = jnp.bfloat16, jnp.float32
    vmem = pl.BlockSpec(memory_space=pltpu.VMEM)
    hbm = pl.BlockSpec(memory_space=pltpu.HBM)
    dma = pltpu.SemaphoreType.DMA
    received = pl.pallas_call(
        functools.partial(kernel, n, segments, steps),
        out_shape=jax.ShapeDtypeStruct((items, width), bf16),
        in_specs=[hbm] * 9,
        out_specs=vmem,
        scratch_shapes=[
            pltpu.VMEM((steps, rows), jnp.int32),
            pltpu.VMEM((1, rows), jnp.int32),
            pltpu.VMEM((2, rows), jnp.int32),
            pltpu.VMEM((steps + 3, rows), f32),
            pltpu.VMEM((1, features), f32),
            pltpu.VMEM((features, query_weight.shape[2]), bf16),
            pltpu.VMEM((2 * kv_columns, features), bf16),
            pltpu.VMEM((out_weight.shape[1], width), bf16),
            pltpu.VMEM((blocks * BLOCK, 2 * HEAD_SIZE), bf16),
            pltpu.VMEM((n, items, width), bf16),
            pltpu.VMEM((items, features), bf16),
            pltpu.VMEM((n, items, heads * HEAD_SIZE), bf16),
            pltpu.VMEM((n, items, 2 * kv_columns), bf16),
            pltpu.VMEM((n, 2 * kv_columns, 2 * HEAD_SIZE), bf16),
            pltpu.VMEM((items, width), bf16),
            pltpu.VMEM((items, width), bf16),
            pltpu.VMEM((items, blocks * BLOCK), f32),
            pltpu.VMEM((items, items), f32),
            pltpu.VMEM((items, HEAD_SIZE), f32),
            pltpu.VMEM((items, HEAD_SIZE), f32),
            pltpu.VMEM((items, 1), f32),
            dma((9,)),
            dma((sends,)), dma((n,)),
            dma((sends,)), dma((n,)),
            dma((sends,)), dma((n,)),
            dma, dma,
        ],
        compiler_params=pltpu.CompilerParams(
            collective_id=0, has_side_effects=True, vmem_limit_bytes=127 * 2**19
        ),
    )(
        step_inputs.reshape(items, width),
        norm_gain,
        query_weight[0],
        kv_weight[0].transpose(1, 2, 0).reshape(2 * kv_columns, features),
        out_weight[0],
        kv_cache.reshape(blocks * BLOCK, 2 * HEAD_SIZE),
        parents,
        prefix_len[None, :],
        block_table.T,
    )
    return received.reshape(1, steps, rows, width)


def solution(mesh):
    return jax.shard_map(
        functools.partial(per_device, mesh.shape["tensor"], mesh.shape["segment"]),
        mesh=mesh,
        in_specs=(
            P(None, None, "tensor"),
            P("segment", None),
            P("segment", None, "tensor"),
            P("segment", None, None, "tensor"),
            P("segment", None, "tensor"),
            P("segment", "tensor", None, None, None),
            P(),
            P(),
            P(),
        ),
        out_specs=P("segment", None, None, "tensor"),
        check_vma=False,
    )
```
